512 devices in a mesh: slab: 256 (over x, z, y), rhs: 2 (over core).
Axes of the slice: x: 4, y: 4, z: 16, core: 2. Of those that a mesh axis runs over, the one named last changes fastest.
Arguments:
- right_spike: float32 [262144, 256], P('slab'), may hold values from -1.1 to 1.1
- left_spike: float32 [262144, 256], P('slab'), may hold values from -1.1 to 1.1
- local_rhs: float32 [64, 262144], P('rhs', 'slab'), may hold values from -2 to 2
Outputs:
- solution: float32 [64, 262144], P('rhs', 'slab')
The draws below stay inside these ranges and needn't reach their ends.
All inputs are finite; a program needn't handle non-finite values.
Results may differ from the reference program's by a relative error of at most 0.0001.
Values sent between devices are 32-bit elements; how exact they have to be, the bound alone decides.
A program may use at most 64 MiB of HBM per device.

```python
import math
import jax
import jax.numpy as jnp
from jax import lax

BLOCK = 256
SLABS = 4
PARTS_SIZE = 256
LEVELS = 8
RHS = 64


def spike_blocks(noise, diagonal, top_scale, bottom_scale):
    identity = jnp.eye(BLOCK, dtype=jnp.float32)
    scaled = noise / math.sqrt(BLOCK)
    tip_blocks = diagonal[..., None] * identity + 0.16 * scaled
    interior = 0.5 * scaled
    slab_number = jnp.arange(SLABS)[None, :, None, None]
    blocks = jnp.where(slab_number == 0, -top_scale * tip_blocks, jnp.where(slab_number == SLABS - 1, -bottom_scale * tip_blocks, interior))
    return blocks.reshape(PARTS_SIZE * SLABS * BLOCK, BLOCK)


def draw_right_spike(key, part):
    key = jax.random.fold_in(key, 5)
    noise_key, diagonal_key = jax.random.split(key)
    array_shape = (PARTS_SIZE, SLABS, BLOCK, BLOCK)
    noise = jnp.clip(jax.random.normal(noise_key, array_shape, jnp.float32), -4.0, 4.0)
    diagonal = jnp.exp(jax.random.uniform(diagonal_key, (PARTS_SIZE, SLABS, BLOCK), jnp.float32, math.log(0.5), math.log(0.97)))
    return spike_blocks(noise, diagonal, 1.0, 0.006)


def draw_left_spike(key, part):
    key = jax.random.fold_in(key, 7)
    noise_key, diagonal_key = jax.random.split(key)
    array_shape = (PARTS_SIZE, SLABS, BLOCK, BLOCK)
    noise = jnp.clip(jax.random.normal(noise_key, array_shape, jnp.float32), -4.0, 4.0)
    diagonal = jnp.exp(jax.random.uniform(diagonal_key, (PARTS_SIZE, SLABS, BLOCK), jnp.float32, math.log(0.5), math.log(0.97)))
    return spike_blocks(noise, diagonal, 0.006, 1.0)


def draw_local_rhs(key, part):
    key = jax.random.fold_in(key, 17)
    array_shape = (RHS, PARTS_SIZE * SLABS * BLOCK)
    return jnp.clip(0.5 * jax.random.normal(key, array_shape, jnp.float32), -2.0, 2.0)


def setup_inputs(seed: int = 0) -> dict:
    seeds = jax.random.split(jax.random.key(seed), 4)
    return {
        "right_spike": draw_right_spike(jax.random.fold_in(seeds[3], 71), 0),
        "left_spike": draw_left_spike(jax.random.fold_in(seeds[3], 71), 0),
        "local_rhs": draw_local_rhs(jax.random.fold_in(seeds[3], 71), 0),
    }


def product(left, right):
    return jnp.matmul(left, right, precision=lax.Precision.HIGHEST)

def reference(right_spike, left_spike, local_rhs):
    part_rows = SLABS * BLOCK
    spikes_right = right_spike.reshape(PARTS_SIZE, part_rows, BLOCK)
    spikes_left = left_spike.reshape(PARTS_SIZE, part_rows, BLOCK)
    sources = jnp.transpose(local_rhs.reshape(RHS, PARTS_SIZE, part_rows), (1, 2, 0))
    tips = [spikes_right[:, :BLOCK], spikes_right[:, part_rows - BLOCK:], spikes_left[:, :BLOCK], spikes_left[:, part_rows - BLOCK:], sources[:, :BLOCK], sources[:, part_rows - BLOCK:]]
    identity = jnp.eye(BLOCK, dtype=jnp.float32)
    records = []
    for section_index in range(LEVELS):
        far_right, near_right, near_left, far_left, source_top, source_bottom = [entry[0::2] for entry in tips]
        other_far_right, other_near_right, other_near_left, other_far_left, other_top, other_bottom = [entry[1::2] for entry in tips]
        kernel = identity - product(near_right, other_near_left)
        right_weight = jnp.linalg.solve(kernel, -product(near_right, other_far_right))
        left_weight = jnp.linalg.solve(kernel, far_left)
        middle_source = jnp.linalg.solve(kernel, source_bottom - product(near_right, other_top))
        next_right = other_far_right - product(other_near_left, right_weight)
        next_left = product(other_near_left, left_weight)
        next_source = other_top - product(other_near_left, middle_source)
        records.append((middle_source, next_source, right_weight, left_weight, next_right, next_left))
        tips = [-product(far_right, next_right), other_near_right - product(other_far_left, right_weight), near_left + product(far_right, next_left), -product(other_far_left, left_weight), source_top - product(far_right, next_source), other_bottom - product(other_far_left, middle_source)]
    left_edge = jnp.zeros((1, BLOCK, RHS), jnp.float32)
    right_edge = jnp.zeros((1, BLOCK, RHS), jnp.float32)
    for section_index in reversed(range(LEVELS)):
        middle_source, next_source, right_weight, left_weight, next_right, next_left = records[section_index]
        middle_left = middle_source - product(right_weight, right_edge) - product(left_weight, left_edge)
        middle_right = next_source - product(next_right, right_edge) + product(next_left, left_edge)
        left_edge = jnp.stack([left_edge, middle_left], axis=1).reshape(-1, BLOCK, RHS)
        right_edge = jnp.stack([middle_right, right_edge], axis=1).reshape(-1, BLOCK, RHS)
    result = sources - product(spikes_right, right_edge) - product(spikes_left, left_edge)
    return jnp.transpose(result, (2, 0, 1)).reshape(RHS, PARTS_SIZE * part_rows)
```

```python
import functools
import jax
import jax.numpy as jnp
from jax import lax
from jax.experimental import pallas as pl
from jax.experimental.pallas import tpu as pltpu
from jax.sharding import PartitionSpec as P

MESH = pl.DeviceIdType.MESH


def split(x):
    high = x.astype(jnp.bfloat16)
    return high, (x - high.astype(jnp.float32)).astype(jnp.bfloat16)


def mm(left, right):
    left_high, left_low = left
    right_high, right_low = right
    dot = functools.partial(jnp.dot, preferred_element_type=jnp.float32)
    return dot(left_high, right_high) + (dot(left_high, right_low) + dot(left_low, right_high))


def kernel(
    levels, tips, sources, out,
    mate, cross, own, gs, goth, zrec, yrec, ysrc, trec, ebuf, esrc,
    msend, mrecv, csend, crecv, fsend, frecv, osend, orecv, gsend, grecv,
    zsend, zrecv, ysend, yrecv, vsend, vrecv, esend, erecv,
):
    s = lax.axis_index("slab")
    c = lax.axis_index("rhs")
    o = 1 - c
    block = tips.shape[1]
    half_size = block // 2
    half = pl.ds(pl.multiple_of(c * half_size, half_size), half_size)
    top = levels - 1

    def roles(d):
        p = lax.div(d, 3)
        q = lax.div(2 * d, 3)
        off = lax.rem(s, d)
        h = lax.rem(lax.div(s, d), 2)
        act_off = q + h * (p - q)
        ret_off = p + h * (q - p)
        base = s - off
        active = off == act_off
        retiring = jnp.logical_and(off == ret_off, p != q)
        partner = base + (1 - 2 * h) * d + ret_off
        return active, retiring, partner, base + act_off, base + ret_off

    def remote(src, dst, send, recv, slab, core):
        return pltpu.make_async_remote_copy(
            src_ref=src, dst_ref=dst, send_sem=send, recv_sem=recv,
            device_id=(slab, core), device_id_type=MESH,
        )

    def mate_copy(k, j):
        ref = mate.at[k, j, half]
        return remote(ref, ref, msend.at[k, j], mrecv.at[k, j], s, o)

    def cross_copy(k, j, partner):
        return remote(
            mate.at[k, j, half], cross.at[k, j, half], csend.at[k, j], crecv.at[k, j], partner, c
        )

    def cross_forward(k, j):
        ref = cross.at[k, j, half]
        return remote(ref, ref, fsend.at[k, j], frecv.at[k, j], s, o)

    def own_copy(k, j, target):
        return remote(
            mate.at[k, j, half], own.at[k, j], osend.at[k, j], orecv.at[k, j], target, c
        )

    def source_copy(k, j, partner):
        return remote(gs.at[k, j], goth.at[k, j], gsend.at[k, j], grecv.at[k, j], partner, c)

    def z_copy(k):
        ref = zrec.at[k, half]
        return remote(ref, ref, zsend.at[k], zrecv.at[k], s, o)

    def y_copy(k, partner):
        return remote(ysrc.at[k], yrec.at[k, half], ysend.at[k], yrecv.at[k], partner, c)

    def y_forward(k):
        ref = yrec.at[k, half]
        return remote(ref, ref, vsend.at[k], vrecv.at[k], s, o)

    def edge_copy(k, target):
        return remote(esrc.at[k], ebuf.at[k - 1], esend.at[k], erecv.at[k], target, c)

    barrier = pltpu.get_barrier_semaphore()

    def greet(slab, core):
        pl.semaphore_signal(barrier, inc=1, device_id=(slab, core), device_id_type=MESH)

    greet(s, o)
    greeted = 1
    for k in range(levels):
        active, retiring, partner, target, retiree = roles(2**k)

        @pl.when(active)
        def _():
            greet(partner, c)
            if k > 0:
                greet(retiree, c)

        greeted = greeted + jnp.where(active, 2 if k > 0 else 1, 0)
        if k > 0:

            @pl.when(retiring)
            def _():
                greet(target, c)

            greeted = greeted + jnp.where(retiring, 1, 0)

    h0 = lax.rem(s, 2)
    for j in range(2):
        mate[0, j] = tips[2 * (1 - h0) + j]
        own[0, j] = tips[2 * h0 + j, half]
    gs[0, 0] = sources[1 - h0]
    gs[0, 1] = sources[h0]
    pl.semaphore_wait(barrier, greeted)

    first_partner = roles(1)[2]
    cross_copy(0, 0, first_partner).start()
    source_copy(0, 0, first_partner).start()
    cross_copy(0, 1, first_partner).start()
    source_copy(0, 1, first_partner).start()

    def solved(rows, coupling):
        power = split(coupling)
        rows = rows + mm(split(rows), power)
        for _ in range(3):
            power = split(mm(power, power))
            rows = rows + mm(split(rows), power)
        return rows

    def up(k, d):
        active, _, partner, _, retiree = roles(d)
        next_active, next_retiring, next_partner, next_target, _ = roles(2 * d)
        below_top = k + 1 < top

        @pl.when(active)
        def _():
            cross_copy(k, 0, partner).wait_recv()
            cross_forward(k, 0).start()
            source_copy(k, 0, partner).wait_recv()

            @pl.when(k > 0)
            def _():
                mate_copy(k, 0).wait_recv()
                own_copy(k, 1, retiree).wait_recv()

            mate_near = split(mate[k, 0])
            rhs = gs[k, 0] - mm(split(goth[k, 0]), mate_near)
            cross_forward(k, 0).wait_recv()
            cross_near = split(cross[k, 0])
            coupling = mm(cross_near, mate_near)
            rows = jnp.concatenate([own[k, 1], rhs], axis=0)
            y = solved(rows, coupling)
            y_parts = split(y)
            z = mm(y_parts, cross_near)
            z_own = z[:half_size]
            t = goth[k, 0] - z[half_size:]
            trec[k] = t
            ysrc[k] = y[:half_size]
            zrec[k, half] = z_own

            cross_copy(k, 1, partner).wait_recv()
            cross_forward(k, 1).start()
            cross_copy(k, 0, partner).wait_send()
            cross_copy(k, 1, partner).wait_send()

            @pl.when(k > 0)
            def _():
                y_copy(k - 1, roles(lax.div(d, 2))[2]).start()
                mate_copy(k, 1).wait_recv()
                own_copy(k, 0, retiree).wait_recv()

            near = jnp.concatenate([own[k, 0], gs[k, 1]], axis=0) + mm(
                split(jnp.concatenate([z_own, -t], axis=0)), split(mate[k, 1])
            )
            mate[k + 1, 0, half] = near[:half_size]
            gs[k + 1, 0] = near[half_size:]

            @pl.when(next_active)
            def _():
                cross_copy(k + 1, 0, next_partner).start()
                mate_copy(k + 1, 0).start()
                source_copy(k + 1, 0, next_partner).start()

            @pl.when(jnp.logical_and(next_retiring, below_top))
            def _():
                own_copy(k + 1, 0, next_target).start()

            source_copy(k, 1, partner).wait_recv()
            cross_forward(k, 1).wait_recv()
            product = mm(y_parts, split(cross[k, 1]))
            mate[k + 1, 1, half] = -product[:half_size]
            gs[k + 1, 1] = goth[k, 1] - product[half_size:]

            @pl.when(jnp.logical_and(next_active, below_top))
            def _():
                cross_copy(k + 1, 1, next_partner).start()
                mate_copy(k + 1, 1).start()
                source_copy(k + 1, 1, next_partner).start()

            @pl.when(jnp.logical_and(next_retiring, below_top))
            def _():
                own_copy(k + 1, 1, next_target).start()

            z_copy(k).start()

            @pl.when(jnp.logical_and(next_retiring, below_top))
            def _():
                own_copy(k + 1, 0, next_target).wait_send()
                own_copy(k + 1, 1, next_target).wait_send()

            @pl.when(next_retiring)
            def _():
                y_copy(k, partner).start()

        return 2 * d

    lax.fori_loop(0, top, up, jnp.int32(1))

    def forward_y(k, d):
        active, _, partner, _, _ = roles(d)

        @pl.when(active)
        def _():
            y_copy(k, partner).wait_recv()
            y_forward(k).start()

        return 2 * d

    lax.fori_loop(0, top - 1, forward_y, jnp.int32(1))

    top_active, _, top_partner, _, top_retiree = roles(2**top)

    @pl.when(top_active)
    def _():
        cross_copy(top, 0, top_partner).wait_recv()
        cross_forward(top, 0).start()
        source_copy(top, 0, top_partner).wait_recv()
        cross_copy(top, 0, top_partner).wait_send()
        y_copy(top - 1, roles(2 ** (top - 1))[2]).start()
        mate_copy(top, 0).wait_recv()
        mate_near = split(mate[top, 0])
        rhs = gs[top, 0] - mm(split(goth[top, 0]), mate_near)
        cross_forward(top, 0).wait_recv()
        cross_near = split(cross[top, 0])
        coupling = mm(cross_near, mate_near)
        solution_rows = solved(rhs, coupling)
        t = goth[top, 0] - mm(split(solution_rows), cross_near)
        esrc[top, 0] = jnp.zeros_like(t)
        esrc[top, 1] = t
        edge_copy(top, top_retiree).start()
        ebuf[top - 1, 0] = t
        ebuf[top - 1, 1] = jnp.zeros_like(t)

    forward_y(top - 1, 2 ** (top - 1))

    def down(index, d):
        k = top - 1 - index
        active, _, _, _, retiree = roles(d)
        _, was_retiring, _, _, _ = roles(2 * d)

        @pl.when(active)
        def _():
            z_copy(k).wait_recv()
            y_forward(k).wait_recv()
            z_parts = split(zrec[k])
            y_parts = split(yrec[k])

            @pl.when(was_retiring)
            def _():
                edge_copy(k + 1, s).wait_recv()

            own_edge = ebuf[k, 0]
            other_edge = ebuf[k, 1]
            new = trec[k] + mm(split(own_edge), z_parts) - mm(split(other_edge), y_parts)

            @pl.when(k > 0)
            def _():
                esrc[k, 0] = own_edge
                esrc[k, 1] = new
                edge_copy(k, retiree).start()
                ebuf[k - 1, 0] = new
                ebuf[k - 1, 1] = own_edge

            @pl.when(k == 0)
            def _():
                out[h0] = own_edge
                out[1 - h0] = new

        return lax.div(d, 2)

    lax.fori_loop(0, top, down, jnp.int32(2 ** (top - 1)))

    def finish(k, d):
        active, _, partner, _, retiree = roles(d)

        @pl.when(active)
        def _():
            source_copy(k, 0, partner).wait_send()
            cross_forward(k, 0).wait_send()

            @pl.when(k > 0)
            def _():
                mate_copy(k, 0).wait_send()
                edge_copy(k, retiree).wait_send()

            @pl.when(k < top)
            def _():
                source_copy(k, 1, partner).wait_send()
                cross_forward(k, 1).wait_send()
                z_copy(k).wait_send()
                y_copy(k, partner).wait_send()
                y_forward(k).wait_send()

            @pl.when(jnp.logical_and(k > 0, k < top))
            def _():
                mate_copy(k, 1).wait_send()

        return 2 * d

    lax.fori_loop(0, levels, finish, jnp.int32(1))


def local(right_spike, left_spike, local_rhs):
    block = right_spike.shape[1]
    part_rows = right_spike.shape[0]
    columns = local_rhs.shape[0]
    levels = lax.axis_size("slab").bit_length() - 1
    last = part_rows - block
    tips = jnp.stack(
        [left_spike[:block].T, left_spike[last:].T, right_spike[last:].T, right_spike[:block].T]
    )
    sources = jnp.stack([local_rhs[:, :block], local_rhs[:, last:]])
    half = block // 2
    f32 = jnp.float32
    pair = pltpu.SemaphoreType.DMA((levels, 2))
    one = pltpu.SemaphoreType.DMA((levels,))
    vmem = pl.BlockSpec(memory_space=pltpu.VMEM)
    edges = pl.pallas_call(
        functools.partial(kernel, levels),
        out_shape=jax.ShapeDtypeStruct((2, columns, block), f32),
        in_specs=[vmem, vmem],
        out_specs=vmem,
        scratch_shapes=[
            pltpu.VMEM((levels, 2, block, block), f32),
            pltpu.VMEM((levels, 2, block, block), f32),
            pltpu.VMEM((levels, 2, half, block), f32),
            pltpu.VMEM((levels, 2, columns, block), f32),
            pltpu.VMEM((levels, 2, columns, block), f32),
            pltpu.VMEM((levels, block, block), f32),
            pltpu.VMEM((levels, block, block), f32),
            pltpu.VMEM((levels, half, block), f32),
            pltpu.VMEM((levels, columns, block), f32),
            pltpu.VMEM((levels, 2, columns, block), f32),
            pltpu.VMEM((levels, 2, columns, block), f32),
        ]
        + [pair] * 10
        + [one] * 8,
        compiler_params=pltpu.CompilerParams(
            collective_id=0, has_side_effects=True, vmem_limit_bytes=40 * 2**20
        ),
    )(tips, sources)

    def against(rows, matrix):
        return lax.dot_general(
            rows,
            matrix,
            (((1,), (1,)), ((), ())),
            precision=lax.Precision.HIGH,
            preferred_element_type=f32,
        )

    return local_rhs - against(edges[1], right_spike) - against(edges[0], left_spike)


def solution(mesh):
    return jax.shard_map(
        local,
        mesh=mesh,
        in_specs=(P("slab", None), P("slab", None), P("rhs", "slab")),
        out_specs=P("rhs", "slab"),
        check_vma=False,
    )
```

```python
import functools
import jax
import jax.numpy as jnp
from jax import lax
from jax.experimental import pallas as pl
from jax.experimental.pallas import tpu as pltpu
from jax.sharding import PartitionSpec as P

MESH = pl.DeviceIdType.MESH


def split(x):
    high = x.astype(jnp.bfloat16)
    return high, (x - high.astype(jnp.float32)).astype(jnp.bfloat16)


def mm(left, right):
    left_high, left_low = left
    right_high, right_low = right
    return jnp.dot(
        jnp.concatenate([left_high, left_high, left_low], axis=1),
        jnp.concatenate([right_high, right_low, right_high], axis=0),
        preferred_element_type=jnp.float32,
    )


def places(levels, left_level, outer_level):
    p = q = 0
    rows = []
    for k in range(levels):
        d = 2**k
        if k == left_level and k < levels - 1:
            rows.append((d, p, p, q, q, 0, 1))
            p, q = p, d + p
        elif k == outer_level and k < levels - 1:
            rows.append((d, p, q, q, p, 0, 0))
            p, q = p, d + q
        else:
            rows.append((d, q, p, p, q, 1, 1))
            p, q = q, d + p
    return rows


LEFT_LEVEL = 2
OUTER_LEVEL = 6


def kernel(
    levels, tips, sources, out,
    side, mate, cross, own, gs, goth, zrec, yrec, ysrc, trec, ebuf, esrc, rec_high, rec_low,
    msend, mrecv, tsend, trecv, csend, crecv, fsend, frecv, osend, orecv, gsend, grecv,
    esend, erecv, kept_sem, zsend, zrecv, ysend, yrecv, vsend, vrecv,
):
    s = lax.axis_index("slab")
    c = lax.axis_index("rhs")
    o = 1 - c
    block = tips.shape[1]
    half_size = block // 2
    half = pl.ds(pl.multiple_of(c * half_size, half_size), half_size)
    other_half = pl.ds(pl.multiple_of(o * half_size, half_size), half_size)
    top = levels - 1
    rows_of = places(levels, LEFT_LEVEL, OUTER_LEVEL)

    def table(k, column):
        values = [row[column] for row in rows_of]
        if isinstance(k, int):
            return values[k]
        value = jnp.int32(values[0])
        for i in range(1, levels):
            value = jnp.where(k == i, values[i], value)
        return value

    def roles(k):
        d, act0, act1, ret0, ret1, keep0, keep1 = [table(k, i) for i in range(7)]
        off = lax.rem(s, d)
        h = lax.rem(lax.div(s, d), 2)
        act_off = act0 + h * (act1 - act0)
        ret_off = ret0 + h * (ret1 - ret0)
        keep = keep0 + h * (keep1 - keep0)
        base = s - off
        other = base + (1 - 2 * h) * d
        return {
            "active": off == act_off,
            "retiring": jnp.logical_and(off == ret_off, act_off != ret_off),
            "keep": keep,
            "keeps": keep == 1,
            "target": base + act_off,
            "retiree": base + ret_off,
            "partner": other + act1 + h * (act0 - act1),
            "other_retiree": other + ret1 + h * (ret0 - ret1),
        }

    def both(*conditions):
        return functools.reduce(jnp.logical_and, conditions)

    def remote(src, dst, send, recv, slab, core):
        return pltpu.make_async_remote_copy(
            src_ref=src, dst_ref=dst, send_sem=send, recv_sem=recv,
            device_id=(slab, core), device_id_type=MESH,
        )

    def mate_copy(k, j, rows=half):
        ref = mate.at[k, j, rows]
        return remote(ref, ref, msend.at[k, j], mrecv.at[k, j], s, o)

    def mate_send(k, j, target):
        return remote(
            side.at[k, j], mate.at[k, j, half], tsend.at[k, j], trecv.at[k, j], target, c
        )

    def cross_copy(k, j, partner):
        return remote(
            side.at[k, j], cross.at[k, j, half], csend.at[k, j], crecv.at[k, j], partner, c
        )

    def cross_forward(k, j, rows=half):
        ref = cross.at[k, j, rows]
        return remote(ref, ref, fsend.at[k, j], frecv.at[k, j], s, o)

    def own_copy(k, j, target):
        return remote(side.at[k, j], own.at[k, j], osend.at[k, j], orecv.at[k, j], target, c)

    def own_keep(k, j):
        return pltpu.make_async_copy(side.at[k, j], own.at[k, j], kept_sem.at[k, j])

    def source_copy(k, j, partner):
        return remote(gs.at[k, j], goth.at[k, j], gsend.at[k, j], grecv.at[k, j], partner, c)

    def z_copy(k, rows=half):
        ref = zrec.at[k, rows]
        return remote(ref, ref, zsend.at[k], zrecv.at[k], s, o)

    def y_copy(k, partner):
        return remote(ysrc.at[k], yrec.at[k, half], ysend.at[k], yrecv.at[k], partner, c)

    def y_forward(k, rows=half):
        ref = yrec.at[k, rows]
        return remote(ref, ref, vsend.at[k], vrecv.at[k], s, o)

    def old_edge_copy(k, keep, target):
        return remote(
            ebuf.at[k, 0], ebuf.at[k - 1, 1 - keep], esend.at[k, 0], erecv.at[k, 0], target, c
        )

    def new_edge_copy(k, keep, target):
        return remote(
            esrc.at[k], ebuf.at[k - 1, keep], esend.at[k, 1], erecv.at[k, 1], target, c
        )

    barrier = pltpu.get_barrier_semaphore()

    def greet(slab, core):
        pl.semaphore_signal(barrier, inc=1, device_id=(slab, core), device_id_type=MESH)

    greet(s, o)
    greet(roles(0)["partner"], c)
    greeted = 2
    for k in range(1, levels):
        r = roles(k)

        @pl.when(r["active"])
        def _():
            greet(r["retiree"], c)

        @pl.when(r["retiring"])
        def _():
            greet(r["target"], c)

        takes_part = jnp.logical_or(r["active"], r["retiring"])

        @pl.when(takes_part)
        def _():
            greet(r["partner"], c)
            greet(r["other_retiree"], c)

        greeted = greeted + jnp.where(takes_part, 3, 0)

    h0 = lax.rem(s, 2)
    for j in range(2):
        mate[0, j] = tips[2 * (1 - h0) + j]
        side[0, j] = tips[2 * (1 - h0) + j, half]
        own[0, j] = tips[2 * h0 + j, half]
    gs[0, 0] = sources[1 - h0]
    gs[0, 1] = sources[h0]
    pl.semaphore_wait(barrier, greeted)

    first_partner = roles(0)["partner"]
    for j in range(2):
        cross_copy(0, j, first_partner).start()
        source_copy(0, j, first_partner).start()

    def solved(rows, coupling):
        power = split(coupling)
        rows = rows + mm(split(rows), power)
        for _ in range(2):
            power = split(mm(power, power))
            rows = rows + mm(split(rows), power)
        dot = functools.partial(jnp.dot, preferred_element_type=jnp.float32)
        last = dot(power[0], power[0]).astype(jnp.bfloat16)
        return rows + dot(rows.astype(jnp.bfloat16), last)

    def send_side(k, j, r, value):
        below_top = k < top
        retiring = r["retiring"] if j == 0 else both(r["retiring"], below_top)
        active = r["active"] if j == 0 else both(r["active"], below_top)
        keeps = r["keeps"]

        @pl.when(both(active, keeps))
        def _():
            cross_copy(k, j, r["partner"]).start()
            mate[k, j, half] = value
            mate_copy(k, j).start()
            source_copy(k, j, r["partner"]).start()

        @pl.when(both(active, jnp.logical_not(keeps)))
        def _():
            own_keep(k, j).start()

        @pl.when(both(retiring, keeps, below_top))
        def _():
            own_copy(k, j, r["target"]).start()

        @pl.when(both(retiring, jnp.logical_not(keeps)))
        def _():
            mate_send(k, j, r["target"]).start()
            cross_copy(k, j, r["partner"]).start()
            source_copy(k, j, r["partner"]).start()

    def up(k, carry):
        r = roles(k)
        following = roles(k + 1)
        keep = r["keep"]
        partner = r["partner"]
        retiree = r["retiree"]
        moved = both(k > 0, jnp.logical_not(r["keeps"]))
        kept = both(k > 0, r["keeps"])

        @pl.when(r["active"])
        def _():
            @pl.when(moved)
            def _():
                mate_send(k, 0, r["target"]).wait_recv()
                mate_copy(k, 0).start()

            cross_copy(k, 0, partner).wait_recv()
            cross_forward(k, 0).start()
            source_copy(k, 0, partner).wait_recv()

            @pl.when(k > 0)
            def _():
                mate_copy(k, 0, other_half).wait_recv()

            @pl.when(kept)
            def _():
                own_copy(k, 1, retiree).wait_recv()

            @pl.when(moved)
            def _():
                own_keep(k, 1).wait()

            mate_near = split(mate[k, 0])
            rhs = gs[k, 1 - keep] - mm(split(goth[k, 0]), mate_near)
            cross_forward(k, 0, other_half).wait_recv()
            cross_near = split(cross[k, 0])
            coupling = mm(cross_near, mate_near)
            y = solved(jnp.concatenate([own[k, 1], rhs], axis=0), coupling)
            y_parts = split(y)
            z = mm(y_parts, cross_near)
            z_own = z[:half_size]
            t = goth[k, 0] - z[half_size:]
            trec[k] = t
            ysrc[k] = y[:half_size]
            zrec[k, half] = z_own

            @pl.when(moved)
            def _():
                mate_send(k, 1, r["target"]).wait_recv()
                mate_copy(k, 1).start()

            @pl.when(k > 0)
            def _():
                mate_copy(k, 1, other_half).wait_recv()

            @pl.when(kept)
            def _():
                own_copy(k, 0, retiree).wait_recv()

            @pl.when(moved)
            def _():
                own_keep(k, 0).wait()

            near = jnp.concatenate([own[k, 0], gs[k, keep]], axis=0) + mm(
                split(jnp.concatenate([z_own, -t], axis=0)), split(mate[k, 1])
            )
            side[k + 1, 0] = near[:half_size]
            gs[k + 1, 0] = near[half_size:]
            send_side(k + 1, 0, following, near[:half_size])

            cross_copy(k, 1, partner).wait_recv()
            cross_forward(k, 1).start()
            source_copy(k, 1, partner).wait_recv()
            cross_forward(k, 1, other_half).wait_recv()
            product = mm(y_parts, split(cross[k, 1]))
            side[k + 1, 1] = -product[:half_size]
            gs[k + 1, 1] = goth[k, 1] - product[half_size:]
            send_side(k + 1, 1, following, -product[:half_size])
            z_copy(k).start()

            @pl.when(both(following["retiring"], k + 1 < top))
            def _():
                @pl.when(following["keeps"])
                def _():
                    for j in range(2):
                        own_copy(k + 1, j, following["target"]).wait_send()

                @pl.when(jnp.logical_not(following["keeps"]))
                def _():
                    for j in range(2):
                        mate_send(k + 1, j, following["target"]).wait_send()
                        cross_copy(k + 1, j, following["partner"]).wait_send()

            y_copy(k, partner).start()

        return carry

    lax.fori_loop(0, top, up, 0)

    def forward_y(k, carry):
        r = roles(k)

        @pl.when(r["active"])
        def _():
            y_copy(k, r["partner"]).wait_recv()
            y_forward(k).start()

        return carry

    lax.fori_loop(0, top - 1, forward_y, 0)

    r_top = roles(top)

    @pl.when(r_top["active"])
    def _():
        cross_copy(top, 0, r_top["partner"]).wait_recv()
        cross_forward(top, 0).start()
        source_copy(top, 0, r_top["partner"]).wait_recv()
        mate_copy(top, 0, other_half).wait_recv()
        mate_near = split(mate[top, 0])
        rhs = gs[top, 0] - mm(split(goth[top, 0]), mate_near)
        cross_forward(top, 0, other_half).wait_recv()
        cross_near = split(cross[top, 0])
        coupling = mm(cross_near, mate_near)
        t = goth[top, 0] - mm(split(solved(rhs, coupling)), cross_near)
        ebuf[top, 0] = jnp.zeros_like(t)
        esrc[top] = t
        new_edge_copy(top, 1, r_top["retiree"]).start()
        old_edge_copy(top, 1, r_top["retiree"]).start()
        ebuf[top - 1, 0] = t
        ebuf[top - 1, 1] = jnp.zeros_like(t)

    forward_y(top - 1, 0)

    def down(index, carry):
        k = top - 1 - index
        r = roles(k)
        above = roles(k + 1)
        keep = r["keep"]

        @pl.when(r["active"])
        def _():
            z_copy(k, other_half).wait_recv()
            y_forward(k, other_half).wait_recv()
            for part, rec in enumerate((zrec, yrec)):
                high, low = split(rec[k])
                rec_high[part * block : (part + 1) * block] = high
                rec_low[part * block : (part + 1) * block] = low

            @pl.when(above["retiring"])
            def _():
                old_edge_copy(k + 1, above["keep"], s).wait_recv()
                new_edge_copy(k + 1, above["keep"], s).wait_recv()

            @pl.when(k > 0)
            def _():
                old_edge_copy(k, keep, r["retiree"]).start()

            own_edge = ebuf[k, 0]
            high, low = split(jnp.concatenate([own_edge, -ebuf[k, 1]], axis=1))
            dot = functools.partial(jnp.dot, preferred_element_type=jnp.float32)
            columns = own_edge.shape[0]
            stacked = dot(jnp.concatenate([high, low], axis=0), rec_high[...])
            new = trec[k] + (
                stacked[:columns] + (stacked[columns:] + dot(high, rec_low[...]))
            )

            @pl.when(k > 0)
            def _():
                esrc[k] = new
                new_edge_copy(k, keep, r["retiree"]).start()
                ebuf[k - 1, 1 - keep] = new
                ebuf[k - 1, keep] = own_edge

            @pl.when(k == 0)
            def _():
                out[h0] = own_edge
                out[1 - h0] = new

        return carry

    lax.fori_loop(0, top, down, 0)

    def finish(k, carry):
        r = roles(k)
        keeps = r["keeps"]
        below_top = k < top
        sends_cross = jnp.logical_or(
            both(r["active"], keeps), both(r["retiring"], jnp.logical_not(keeps))
        )

        @pl.when(sends_cross)
        def _():
            source_copy(k, 0, r["partner"]).wait_send()

            @pl.when(below_top)
            def _():
                source_copy(k, 1, r["partner"]).wait_send()

        @pl.when(both(r["active"], keeps))
        def _():
            cross_copy(k, 0, r["partner"]).wait_send()

            @pl.when(below_top)
            def _():
                cross_copy(k, 1, r["partner"]).wait_send()

        @pl.when(r["active"])
        def _():
            cross_forward(k, 0).wait_send()

            @pl.when(k > 0)
            def _():
                mate_copy(k, 0).wait_send()
                old_edge_copy(k, r["keep"], r["retiree"]).wait_send()
                new_edge_copy(k, r["keep"], r["retiree"]).wait_send()

            @pl.when(below_top)
            def _():
                cross_forward(k, 1).wait_send()
                z_copy(k).wait_send()
                y_copy(k, r["partner"]).wait_send()
                y_forward(k).wait_send()

            @pl.when(both(k > 0, below_top))
            def _():
                mate_copy(k, 1).wait_send()

        return carry

    lax.fori_loop(0, levels, finish, 0)


def local(right_spike, left_spike, local_rhs):
    block = right_spike.shape[1]
    part_rows = right_spike.shape[0]
    columns = local_rhs.shape[0]
    levels = lax.axis_size("slab").bit_length() - 1
    last = part_rows - block
    tips = jnp.stack(
        [left_spike[:block].T, left_spike[last:].T, right_spike[last:].T, right_spike[:block].T]
    )
    sources = jnp.stack([local_rhs[:, :block], local_rhs[:, last:]])
    half = block // 2
    f32 = jnp.float32
    pair = pltpu.SemaphoreType.DMA((levels, 2))
    one = pltpu.SemaphoreType.DMA((levels,))
    vmem = pl.BlockSpec(memory_space=pltpu.VMEM)
    edges = pl.pallas_call(
        functools.partial(kernel, levels),
        out_shape=jax.ShapeDtypeStruct((2, columns, block), f32),
        in_specs=[vmem, vmem],
        out_specs=vmem,
        scratch_shapes=[
            pltpu.VMEM((levels, 2, half, block), f32),
            pltpu.VMEM((levels, 2, block, block), f32),
            pltpu.VMEM((levels, 2, block, block), f32),
            pltpu.VMEM((levels, 2, half, block), f32),
            pltpu.VMEM((levels, 2, columns, block), f32),
            pltpu.VMEM((levels, 2, columns, block), f32),
            pltpu.VMEM((levels, block, block), f32),
            pltpu.VMEM((levels, block, block), f32),
            pltpu.VMEM((levels, half, block), f32),
            pltpu.VMEM((levels, columns, block), f32),
            pltpu.VMEM((levels, 2, columns, block), f32),
            pltpu.VMEM((levels, columns, block), f32),
            pltpu.VMEM((2 * block, block), jnp.bfloat16),
            pltpu.VMEM((2 * block, block), jnp.bfloat16),
        ]
        + [pair] * 15
        + [one] * 6,
        compiler_params=pltpu.CompilerParams(
            collective_id=0, has_side_effects=True, vmem_limit_bytes=40 * 2**20
        ),
    )(tips, sources)

    def against(rows, matrix):
        return lax.dot_general(
            rows,
            matrix,
            (((1,), (1,)), ((), ())),
            precision=lax.Precision.HIGH,
            preferred_element_type=f32,
        )

    return local_rhs - against(edges[1], right_spike) - against(edges[0], left_spike)


def solution(mesh):
    return jax.shard_map(
        local,
        mesh=mesh,
        in_specs=(P("slab", None), P("slab", None), P("rhs", "slab")),
        out_specs=P("rhs", "slab"),
        check_vma=False,
    )
```

```python
import functools
import jax
import jax.numpy as jnp
from jax import lax
from jax.experimental import pallas as pl
from jax.experimental.pallas import tpu as pltpu
from jax.sharding import PartitionSpec as P

MESH = pl.DeviceIdType.MESH


def split(x):
    high = x.astype(jnp.bfloat16)
    return high, (x - high.astype(jnp.float32)).astype(jnp.bfloat16)


def mm(left, right):
    left_high, left_low = left
    right_high, right_low = right
    return jnp.dot(
        jnp.concatenate([left_high, left_high, left_low], axis=1),
        jnp.concatenate([right_high, right_low, right_high], axis=0),
        preferred_element_type=jnp.float32,
    )


def places(levels, left_level, outer_level):
    p = q = 0
    rows = []
    for k in range(levels):
        d = 2**k
        if k == left_level and k < levels - 1:
            rows.append((d, p, p, q, q, 0, 1))
            p, q = p, d + p
        elif k == outer_level and k < levels - 1:
            rows.append((d, p, q, q, p, 0, 0))
            p, q = p, d + q
        else:
            rows.append((d, q, p, p, q, 1, 1))
            p, q = q, d + p
    return rows


LEFT_LEVEL = 2
OUTER_LEVEL = 6


def kernel(
    levels, tips, sources, out,
    side, mate, cross, own, gs, goth, zrec, yrec, ysrc, trec, ebuf, esrc, rec_high, rec_low,
    mate_high, mate_low,
    msend, mrecv, tsend, trecv, csend, crecv, fsend, frecv, osend, orecv, gsend, grecv,
    esend, erecv, kept_sem, zsend, zrecv, ysend, yrecv, vsend, vrecv,
):
    s = lax.axis_index("slab")
    c = lax.axis_index("rhs")
    o = 1 - c
    block = tips.shape[1]
    half_size = block // 2
    half = pl.ds(pl.multiple_of(c * half_size, half_size), half_size)
    other_half = pl.ds(pl.multiple_of(o * half_size, half_size), half_size)
    top = levels - 1
    rows_of = places(levels, LEFT_LEVEL, OUTER_LEVEL)

    def table(k, column):
        values = [row[column] for row in rows_of]
        if isinstance(k, int):
            return values[k]
        value = jnp.int32(values[0])
        for i in range(1, levels):
            value = jnp.where(k == i, values[i], value)
        return value

    def roles(k):
        d, act0, act1, ret0, ret1, keep0, keep1 = [table(k, i) for i in range(7)]
        off = lax.rem(s, d)
        h = lax.rem(lax.div(s, d), 2)
        act_off = act0 + h * (act1 - act0)
        ret_off = ret0 + h * (ret1 - ret0)
        keep = keep0 + h * (keep1 - keep0)
        base = s - off
        other = base + (1 - 2 * h) * d
        return {
            "active": off == act_off,
            "retiring": jnp.logical_and(off == ret_off, act_off != ret_off),
            "keep": keep,
            "keeps": keep == 1,
            "target": base + act_off,
            "retiree": base + ret_off,
            "partner": other + act1 + h * (act0 - act1),
            "other_retiree": other + ret1 + h * (ret0 - ret1),
        }

    def both(*conditions):
        return functools.reduce(jnp.logical_and, conditions)

    def remote(src, dst, send, recv, slab, core):
        return pltpu.make_async_remote_copy(
            src_ref=src, dst_ref=dst, send_sem=send, recv_sem=recv,
            device_id=(slab, core), device_id_type=MESH,
        )

    def mate_copy(k, j, rows=half):
        ref = mate.at[k, j, rows]
        return remote(ref, ref, msend.at[k, j], mrecv.at[k, j], s, o)

    def mate_send(k, j, target):
        return remote(
            side.at[k, j], mate.at[k, j, half], tsend.at[k, j], trecv.at[k, j], target, c
        )

    def cross_copy(k, j, partner):
        return remote(
            side.at[k, j], cross.at[k, j, half], csend.at[k, j], crecv.at[k, j], partner, c
        )

    def cross_forward(k, j, rows=half):
        ref = cross.at[k, j, rows]
        return remote(ref, ref, fsend.at[k, j], frecv.at[k, j], s, o)

    def own_copy(k, j, target):
        return remote(side.at[k, j], own.at[k, j], osend.at[k, j], orecv.at[k, j], target, c)

    def own_keep(k, j):
        return pltpu.make_async_copy(side.at[k, j], own.at[k, j], kept_sem.at[k, j])

    def source_copy(k, j, partner):
        return remote(gs.at[k, j], goth.at[k, j], gsend.at[k, j], grecv.at[k, j], partner, c)

    def z_copy(k, rows=half):
        ref = zrec.at[k, rows]
        return remote(ref, ref, zsend.at[k], zrecv.at[k], s, o)

    def y_copy(k, partner):
        return remote(ysrc.at[k], yrec.at[k, half], ysend.at[k], yrecv.at[k], partner, c)

    def y_forward(k, rows=half):
        ref = yrec.at[k, rows]
        return remote(ref, ref, vsend.at[k], vrecv.at[k], s, o)

    def old_edge_copy(k, keep, target):
        return remote(
            ebuf.at[k, 0], ebuf.at[k - 1, 1 - keep], esend.at[k, 0], erecv.at[k, 0], target, c
        )

    def new_edge_copy(k, keep, target):
        return remote(
            esrc.at[k], ebuf.at[k - 1, keep], esend.at[k, 1], erecv.at[k, 1], target, c
        )

    barrier = pltpu.get_barrier_semaphore()

    def greet(slab, core):
        pl.semaphore_signal(barrier, inc=1, device_id=(slab, core), device_id_type=MESH)

    greet(s, o)
    greet(roles(0)["partner"], c)
    greeted = 2
    for k in range(1, levels):
        r = roles(k)

        @pl.when(r["active"])
        def _():
            greet(r["retiree"], c)

        @pl.when(r["retiring"])
        def _():
            greet(r["target"], c)

        takes_part = jnp.logical_or(r["active"], r["retiring"])

        @pl.when(takes_part)
        def _():
            greet(r["partner"], c)
            greet(r["other_retiree"], c)

        greeted = greeted + jnp.where(takes_part, 3, 0)

    h0 = lax.rem(s, 2)
    for j in range(2):
        mate[0, j] = tips[2 * (1 - h0) + j]
        side[0, j] = tips[2 * (1 - h0) + j, half]
        own[0, j] = tips[2 * h0 + j, half]
    gs[0, 0] = sources[1 - h0]
    gs[0, 1] = sources[h0]
    pl.semaphore_wait(barrier, greeted)

    first_partner = roles(0)["partner"]
    for j in range(2):
        cross_copy(0, j, first_partner).start()
        source_copy(0, j, first_partner).start()

    def inverse_rest(coupling):
        power = split(coupling)
        rest = coupling
        for _ in range(2):
            square = mm(power, power)
            power = split(square)
            rest = rest + square + mm(split(rest), power)
        dot = functools.partial(jnp.dot, preferred_element_type=jnp.float32)
        last = dot(power[0], power[0])
        return rest + last + dot(rest.astype(jnp.bfloat16), last.astype(jnp.bfloat16))

    def send_side(k, j, r, value):
        below_top = k < top
        retiring = r["retiring"] if j == 0 else both(r["retiring"], below_top)
        active = r["active"] if j == 0 else both(r["active"], below_top)
        keeps = r["keeps"]

        @pl.when(both(active, keeps))
        def _():
            cross_copy(k, j, r["partner"]).start()
            mate[k, j, half] = value
            mate_copy(k, j).start()
            source_copy(k, j, r["partner"]).start()

        @pl.when(both(active, jnp.logical_not(keeps)))
        def _():
            own_keep(k, j).start()

        @pl.when(both(retiring, keeps, below_top))
        def _():
            own_copy(k, j, r["target"]).start()

        @pl.when(both(retiring, jnp.logical_not(keeps)))
        def _():
            mate_send(k, j, r["target"]).start()
            cross_copy(k, j, r["partner"]).start()
            source_copy(k, j, r["partner"]).start()

    def up(k, carry):
        r = roles(k)
        following = roles(k + 1)
        keep = r["keep"]
        partner = r["partner"]
        retiree = r["retiree"]
        moved = both(k > 0, jnp.logical_not(r["keeps"]))
        kept = both(k > 0, r["keeps"])

        def split_mate(j):
            mate_high[j], mate_low[j] = split(mate[k, j])

        @pl.when(r["active"])
        def _():
            @pl.when(moved)
            def _():
                mate_send(k, 0, r["target"]).wait_recv()
                mate_copy(k, 0).start()

            @pl.when(k > 0)
            def _():
                mate_copy(k, 0, other_half).wait_recv()

            split_mate(0)

            @pl.when(kept)
            def _():
                mate_copy(k, 1, other_half).wait_recv()

            @pl.when(jnp.logical_not(moved))
            def _():
                split_mate(1)

            cross_copy(k, 0, partner).wait_recv()
            cross_forward(k, 0).start()
            source_copy(k, 0, partner).wait_recv()
            mate_near = mate_high[0], mate_low[0]
            rhs = gs[k, 1 - keep] - mm(split(goth[k, 0]), mate_near)
            cross_forward(k, 0, other_half).wait_recv()
            cross_near = split(cross[k, 0])
            rest = inverse_rest(mm(cross_near, mate_near))

            @pl.when(kept)
            def _():
                own_copy(k, 1, retiree).wait_recv()

            @pl.when(moved)
            def _():
                own_keep(k, 1).wait()

            rows = jnp.concatenate([own[k, 1], rhs], axis=0)
            y = rows + mm(split(rows), split(rest))
            y_parts = split(y)
            cross_copy(k, 1, partner).wait_recv()
            cross_forward(k, 1).start()
            z = mm(y_parts, cross_near)
            z_own = z[:half_size]
            t = goth[k, 0] - z[half_size:]
            trec[k] = t
            ysrc[k] = y[:half_size]
            zrec[k, half] = z_own

            @pl.when(moved)
            def _():
                mate_send(k, 1, r["target"]).wait_recv()
                mate_copy(k, 1).start()
                own_keep(k, 0).wait()
                mate_copy(k, 1, other_half).wait_recv()
                split_mate(1)

            @pl.when(kept)
            def _():
                own_copy(k, 0, retiree).wait_recv()

            near = jnp.concatenate([own[k, 0], gs[k, keep]], axis=0) + mm(
                split(jnp.concatenate([z_own, -t], axis=0)), (mate_high[1], mate_low[1])
            )
            side[k + 1, 0] = near[:half_size]
            gs[k + 1, 0] = near[half_size:]
            send_side(k + 1, 0, following, near[:half_size])

            source_copy(k, 1, partner).wait_recv()
            cross_forward(k, 1, other_half).wait_recv()
            product = mm(y_parts, split(cross[k, 1]))
            side[k + 1, 1] = -product[:half_size]
            gs[k + 1, 1] = goth[k, 1] - product[half_size:]
            send_side(k + 1, 1, following, -product[:half_size])
            z_copy(k).start()

            @pl.when(both(following["retiring"], k + 1 < top))
            def _():
                @pl.when(following["keeps"])
                def _():
                    for j in range(2):
                        own_copy(k + 1, j, following["target"]).wait_send()

                @pl.when(jnp.logical_not(following["keeps"]))
                def _():
                    for j in range(2):
                        mate_send(k + 1, j, following["target"]).wait_send()
                        cross_copy(k + 1, j, following["partner"]).wait_send()

            y_copy(k, partner).start()

        return carry

    lax.fori_loop(0, top, up, 0)

    def forward_y(k, carry):
        r = roles(k)

        @pl.when(r["active"])
        def _():
            y_copy(k, r["partner"]).wait_recv()
            y_forward(k).start()

        return carry

    lax.fori_loop(0, top - 1, forward_y, 0)

    r_top = roles(top)

    @pl.when(r_top["active"])
    def _():
        cross_copy(top, 0, r_top["partner"]).wait_recv()
        cross_forward(top, 0).start()
        source_copy(top, 0, r_top["partner"]).wait_recv()
        mate_copy(top, 0, other_half).wait_recv()
        mate_near = split(mate[top, 0])
        rhs = gs[top, 0] - mm(split(goth[top, 0]), mate_near)
        cross_forward(top, 0, other_half).wait_recv()
        cross_near = split(cross[top, 0])
        coupling = mm(cross_near, mate_near)
        middle = rhs + mm(split(rhs), split(inverse_rest(coupling)))
        t = goth[top, 0] - mm(split(middle), cross_near)
        ebuf[top, 0] = jnp.zeros_like(t)
        esrc[top] = t
        new_edge_copy(top, 1, r_top["retiree"]).start()
        old_edge_copy(top, 1, r_top["retiree"]).start()
        ebuf[top - 1, 0] = t
        ebuf[top - 1, 1] = jnp.zeros_like(t)

    forward_y(top - 1, 0)

    def down(index, carry):
        k = top - 1 - index
        r = roles(k)
        above = roles(k + 1)
        keep = r["keep"]

        @pl.when(r["active"])
        def _():
            z_copy(k, other_half).wait_recv()
            y_forward(k, other_half).wait_recv()
            for part, rec in enumerate((zrec, yrec)):
                high, low = split(rec[k])
                rec_high[part * block : (part + 1) * block] = high
                rec_low[part * block : (part + 1) * block] = low

            @pl.when(above["retiring"])
            def _():
                old_edge_copy(k + 1, above["keep"], s).wait_recv()
                new_edge_copy(k + 1, above["keep"], s).wait_recv()

            @pl.when(k > 0)
            def _():
                old_edge_copy(k, keep, r["retiree"]).start()

            own_edge = ebuf[k, 0]
            high, low = split(jnp.concatenate([own_edge, -ebuf[k, 1]], axis=1))
            dot = functools.partial(jnp.dot, preferred_element_type=jnp.float32)
            columns = own_edge.shape[0]
            stacked = dot(jnp.concatenate([high, low], axis=0), rec_high[...])
            new = trec[k] + (
                stacked[:columns] + (stacked[columns:] + dot(high, rec_low[...]))
            )

            @pl.when(k > 0)
            def _():
                esrc[k] = new
                new_edge_copy(k, keep, r["retiree"]).start()
                ebuf[k - 1, 1 - keep] = new
                ebuf[k - 1, keep] = own_edge

            @pl.when(k == 0)
            def _():
                out[h0] = own_edge
                out[1 - h0] = new

        return carry

    lax.fori_loop(0, top, down, 0)

    def finish(k, carry):
        r = roles(k)
        keeps = r["keeps"]
        below_top = k < top
        sends_cross = jnp.logical_or(
            both(r["active"], keeps), both(r["retiring"], jnp.logical_not(keeps))
        )

        @pl.when(sends_cross)
        def _():
            source_copy(k, 0, r["partner"]).wait_send()

            @pl.when(below_top)
            def _():
                source_copy(k, 1, r["partner"]).wait_send()

        @pl.when(both(r["active"], keeps))
        def _():
            cross_copy(k, 0, r["partner"]).wait_send()

            @pl.when(below_top)
            def _():
                cross_copy(k, 1, r["partner"]).wait_send()

        @pl.when(r["active"])
        def _():
            cross_forward(k, 0).wait_send()

            @pl.when(k > 0)
            def _():
                mate_copy(k, 0).wait_send()
                old_edge_copy(k, r["keep"], r["retiree"]).wait_send()
                new_edge_copy(k, r["keep"], r["retiree"]).wait_send()

            @pl.when(below_top)
            def _():
                cross_forward(k, 1).wait_send()
                z_copy(k).wait_send()
                y_copy(k, r["partner"]).wait_send()
                y_forward(k).wait_send()

            @pl.when(both(k > 0, below_top))
            def _():
                mate_copy(k, 1).wait_send()

        return carry

    lax.fori_loop(0, levels, finish, 0)


def local(right_spike, left_spike, local_rhs):
    block = right_spike.shape[1]
    part_rows = right_spike.shape[0]
    columns = local_rhs.shape[0]
    levels = lax.axis_size("slab").bit_length() - 1
    last = part_rows - block
    tips = jnp.stack(
        [left_spike[:block].T, left_spike[last:].T, right_spike[last:].T, right_spike[:block].T]
    )
    sources = jnp.stack([local_rhs[:, :block], local_rhs[:, last:]])
    half = block // 2
    f32 = jnp.float32
    pair = pltpu.SemaphoreType.DMA((levels, 2))
    one = pltpu.SemaphoreType.DMA((levels,))
    vmem = pl.BlockSpec(memory_space=pltpu.VMEM)
    edges = pl.pallas_call(
        functools.partial(kernel, levels),
        out_shape=jax.ShapeDtypeStruct((2, columns, block), f32),
        in_specs=[vmem, vmem],
        out_specs=vmem,
        scratch_shapes=[
            pltpu.VMEM((levels, 2, half, block), f32),
            pltpu.VMEM((levels, 2, block, block), f32),
            pltpu.VMEM((levels, 2, block, block), f32),
            pltpu.VMEM((levels, 2, half, block), f32),
            pltpu.VMEM((levels, 2, columns, block), f32),
            pltpu.VMEM((levels, 2, columns, block), f32),
            pltpu.VMEM((levels, block, block), f32),
            pltpu.VMEM((levels, block, block), f32),
            pltpu.VMEM((levels, half, block), f32),
            pltpu.VMEM((levels, columns, block), f32),
            pltpu.VMEM((levels, 2, columns, block), f32),
            pltpu.VMEM((levels, columns, block), f32),
            pltpu.VMEM((2 * block, block), jnp.bfloat16),
            pltpu.VMEM((2 * block, block), jnp.bfloat16),
            pltpu.VMEM((2, block, block), jnp.bfloat16),
            pltpu.VMEM((2, block, block), jnp.bfloat16),
        ]
        + [pair] * 15
        + [one] * 6,
        compiler_params=pltpu.CompilerParams(
            collective_id=0, has_side_effects=True, vmem_limit_bytes=40 * 2**20
        ),
    )(tips, sources)

    def against(rows, matrix):
        return lax.dot_general(
            rows,
            matrix,
            (((1,), (1,)), ((), ())),
            precision=lax.Precision.HIGH,
            preferred_element_type=f32,
        )

    return local_rhs - against(edges[1], right_spike) - against(edges[0], left_spike)


def solution(mesh):
    return jax.shard_map(
        local,
        mesh=mesh,
        in_specs=(P("slab", None), P("slab", None), P("rhs", "slab")),
        out_specs=P("rhs", "slab"),
        check_vma=False,
    )
```

```python
import functools
import jax
import jax.numpy as jnp
from jax import lax
from jax.experimental import pallas as pl
from jax.experimental.pallas import tpu as pltpu
from jax.sharding import PartitionSpec as P

MESH = pl.DeviceIdType.MESH


def split(x):
    high = x.astype(jnp.bfloat16)
    return high, (x - high.astype(jnp.float32)).astype(jnp.bfloat16)


def mm(left, right):
    left_high, left_low = left
    right_high, right_low = right
    return jnp.dot(
        jnp.concatenate([left_high, left_high, left_low], axis=1),
        jnp.concatenate([right_high, right_low, right_high], axis=0),
        preferred_element_type=jnp.float32,
    )


def places(levels, left_level, outer_level):
    p = q = 0
    rows = []
    for k in range(levels):
        d = 2**k
        if k == left_level and k < levels - 1:
            rows.append((d, p, p, q, q, 0, 1))
            p, q = p, d + p
        elif k == outer_level and k < levels - 1:
            rows.append((d, p, q, q, p, 0, 0))
            p, q = p, d + q
        else:
            rows.append((d, q, p, p, q, 1, 1))
            p, q = q, d + p
    return rows


LEFT_LEVEL = 2
OUTER_LEVEL = 6


def kernel(
    levels, tips, sources, out,
    side, mate, cross, own, gs, goth, zrec, yrec, ysrc, trec, ebuf, esrc, rec_high, rec_low,
    mate_high, mate_low,
    msend, mrecv, tsend, trecv, csend, crecv, fsend, frecv, osend, orecv, gsend, grecv,
    esend, erecv, kept_sem, zsend, zrecv, ysend, yrecv, vsend, vrecv,
):
    s = lax.axis_index("slab")
    c = lax.axis_index("rhs")
    o = 1 - c
    block = tips.shape[1]
    half_size = block // 2
    half = pl.ds(pl.multiple_of(c * half_size, half_size), half_size)
    other_half = pl.ds(pl.multiple_of(o * half_size, half_size), half_size)
    top = levels - 1
    rows_of = places(levels, LEFT_LEVEL, OUTER_LEVEL)

    def table(k, column):
        values = [row[column] for row in rows_of]
        if isinstance(k, int):
            return values[k]
        value = jnp.int32(values[0])
        for i in range(1, levels):
            value = jnp.where(k == i, values[i], value)
        return value

    def roles(k):
        d, act0, act1, ret0, ret1, keep0, keep1 = [table(k, i) for i in range(7)]
        off = lax.rem(s, d)
        h = lax.rem(lax.div(s, d), 2)
        act_off = act0 + h * (act1 - act0)
        ret_off = ret0 + h * (ret1 - ret0)
        keep = keep0 + h * (keep1 - keep0)
        base = s - off
        other = base + (1 - 2 * h) * d
        return {
            "active": off == act_off,
            "retiring": jnp.logical_and(off == ret_off, act_off != ret_off),
            "keep": keep,
            "keeps": keep == 1,
            "target": base + act_off,
            "retiree": base + ret_off,
            "partner": other + act1 + h * (act0 - act1),
            "other_retiree": other + ret1 + h * (ret0 - ret1),
        }

    def both(*conditions):
        return functools.reduce(jnp.logical_and, conditions)

    def remote(src, dst, send, recv, slab, core):
        return pltpu.make_async_remote_copy(
            src_ref=src, dst_ref=dst, send_sem=send, recv_sem=recv,
            device_id=(slab, core), device_id_type=MESH,
        )

    def mate_copy(k, j, rows=half):
        ref = mate.at[k, j, rows]
        return remote(ref, ref, msend.at[k, j], mrecv.at[k, j], s, o)

    def mate_send(k, j, target):
        return remote(
            side.at[k, j], mate.at[k, j, half], tsend.at[k, j], trecv.at[k, j], target, c
        )

    def cross_copy(k, j, partner):
        return remote(
            side.at[k, j], cross.at[k, j, half], csend.at[k, j], crecv.at[k, j], partner, c
        )

    def cross_forward(k, j, rows=half):
        ref = cross.at[k, j, rows]
        return remote(ref, ref, fsend.at[k, j], frecv.at[k, j], s, o)

    def own_copy(k, j, target):
        return remote(side.at[k, j], own.at[k, j], osend.at[k, j], orecv.at[k, j], target, c)

    def own_keep(k, j):
        return pltpu.make_async_copy(side.at[k, j], own.at[k, j], kept_sem.at[k, j])

    def source_copy(k, j, partner):
        return remote(gs.at[k, j], goth.at[k, j], gsend.at[k, j], grecv.at[k, j], partner, c)

    def z_copy(k, rows=half):
        ref = zrec.at[k, rows]
        return remote(ref, ref, zsend.at[k], zrecv.at[k], s, o)

    def y_copy(k, partner):
        return remote(ysrc.at[k], yrec.at[k, half], ysend.at[k], yrecv.at[k], partner, c)

    def y_forward(k, rows=half):
        ref = yrec.at[k, rows]
        return remote(ref, ref, vsend.at[k], vrecv.at[k], s, o)

    def old_edge_copy(k, keep, target):
        return remote(
            ebuf.at[k, 0], ebuf.at[k - 1, 1 - keep], esend.at[k, 0], erecv.at[k, 0], target, c
        )

    def new_edge_copy(k, keep, target):
        return remote(
            esrc.at[k], ebuf.at[k - 1, keep], esend.at[k, 1], erecv.at[k, 1], target, c
        )

    barrier = pltpu.get_barrier_semaphore()

    def greet(slab, core):
        pl.semaphore_signal(barrier, inc=1, device_id=(slab, core), device_id_type=MESH)

    greet(s, o)
    greet(roles(0)["partner"], c)
    greeted = 2
    for k in range(1, levels):
        r = roles(k)

        @pl.when(r["active"])
        def _():
            greet(r["retiree"], c)

        @pl.when(r["retiring"])
        def _():
            greet(r["target"], c)

        takes_part = jnp.logical_or(r["active"], r["retiring"])

        @pl.when(takes_part)
        def _():
            greet(r["partner"], c)
            greet(r["other_retiree"], c)

        greeted = greeted + jnp.where(takes_part, 3, 0)

    h0 = lax.rem(s, 2)
    for j in range(2):
        mate[0, j] = tips[2 * (1 - h0) + j]
        side[0, j] = tips[2 * (1 - h0) + j, half]
        own[0, j] = tips[2 * h0 + j, half]
    gs[0, 0] = sources[1 - h0]
    gs[0, 1] = sources[h0]
    pl.semaphore_wait(barrier, greeted)

    first_partner = roles(0)["partner"]
    for j in range(2):
        cross_copy(0, j, first_partner).start()
        source_copy(0, j, first_partner).start()

    dot = functools.partial(jnp.dot, preferred_element_type=jnp.float32)

    def approx_rest(coupling):
        first = coupling.astype(jnp.bfloat16)
        square = dot(first, first)
        second = square.astype(jnp.bfloat16)
        rest = coupling + square + dot(first, second)
        fourth = dot(second, second)
        rest = rest + fourth + dot(rest.astype(jnp.bfloat16), fourth.astype(jnp.bfloat16))
        return rest.astype(jnp.bfloat16)

    def refined(rows, rest, coupling):
        start = rows + dot(rows.astype(jnp.bfloat16), rest)
        residual = (rows - start) + mm(split(start), coupling)
        return start + (residual + dot(residual.astype(jnp.bfloat16), rest))

    def send_side(k, j, r, value):
        below_top = k < top
        retiring = r["retiring"] if j == 0 else both(r["retiring"], below_top)
        active = r["active"] if j == 0 else both(r["active"], below_top)
        keeps = r["keeps"]

        @pl.when(both(active, keeps))
        def _():
            cross_copy(k, j, r["partner"]).start()
            mate[k, j, half] = value
            mate_copy(k, j).start()
            source_copy(k, j, r["partner"]).start()

        @pl.when(both(active, jnp.logical_not(keeps)))
        def _():
            own_keep(k, j).start()

        @pl.when(both(retiring, keeps, below_top))
        def _():
            own_copy(k, j, r["target"]).start()

        @pl.when(both(retiring, jnp.logical_not(keeps)))
        def _():
            mate_send(k, j, r["target"]).start()
            cross_copy(k, j, r["partner"]).start()
            source_copy(k, j, r["partner"]).start()

    def up(k, carry):
        r = roles(k)
        following = roles(k + 1)
        keep = r["keep"]
        partner = r["partner"]
        retiree = r["retiree"]
        moved = both(k > 0, jnp.logical_not(r["keeps"]))
        kept = both(k > 0, r["keeps"])

        def split_mate(j):
            mate_high[j], mate_low[j] = split(mate[k, j])

        @pl.when(r["active"])
        def _():
            @pl.when(moved)
            def _():
                mate_send(k, 0, r["target"]).wait_recv()
                mate_copy(k, 0).start()

            @pl.when(k > 0)
            def _():
                mate_copy(k, 0, other_half).wait_recv()

            split_mate(0)

            @pl.when(kept)
            def _():
                mate_copy(k, 1, other_half).wait_recv()

            @pl.when(jnp.logical_not(moved))
            def _():
                split_mate(1)

            cross_copy(k, 0, partner).wait_recv()
            cross_forward(k, 0).start()
            source_copy(k, 0, partner).wait_recv()
            mate_near = mate_high[0], mate_low[0]
            rhs = gs[k, 1 - keep] - mm(split(goth[k, 0]), mate_near)
            cross_forward(k, 0, other_half).wait_recv()
            cross_near = split(cross[k, 0])
            coupling = mm(cross_near, mate_near)
            rest = approx_rest(coupling)
            coupling = split(coupling)

            @pl.when(kept)
            def _():
                own_copy(k, 1, retiree).wait_recv()

            @pl.when(moved)
            def _():
                own_keep(k, 1).wait()

            rows = jnp.concatenate([own[k, 1], rhs], axis=0)
            y = refined(rows, rest, coupling)
            y_parts = split(y)
            cross_copy(k, 1, partner).wait_recv()
            cross_forward(k, 1).start()
            z = mm(y_parts, cross_near)
            z_own = z[:half_size]
            t = goth[k, 0] - z[half_size:]

            @pl.when(moved)
            def _():
                mate_send(k, 1, r["target"]).wait_recv()
                mate_copy(k, 1).start()
                own_keep(k, 0).wait()
                mate_copy(k, 1, other_half).wait_recv()
                split_mate(1)

            @pl.when(kept)
            def _():
                own_copy(k, 0, retiree).wait_recv()

            near = jnp.concatenate([own[k, 0], gs[k, keep]], axis=0) + mm(
                split(jnp.concatenate([z_own, -t], axis=0)), (mate_high[1], mate_low[1])
            )
            side[k + 1, 0] = near[:half_size]
            gs[k + 1, 0] = near[half_size:]
            send_side(k + 1, 0, following, near[:half_size])

            trec[k] = t
            ysrc[k] = y[:half_size]
            zrec[k, half] = z_own
            source_copy(k, 1, partner).wait_recv()
            cross_forward(k, 1, other_half).wait_recv()
            product = mm(y_parts, split(cross[k, 1]))
            side[k + 1, 1] = -product[:half_size]
            gs[k + 1, 1] = goth[k, 1] - product[half_size:]
            send_side(k + 1, 1, following, -product[:half_size])
            z_copy(k).start()

            @pl.when(both(following["retiring"], k + 1 < top))
            def _():
                @pl.when(following["keeps"])
                def _():
                    for j in range(2):
                        own_copy(k + 1, j, following["target"]).wait_send()

                @pl.when(jnp.logical_not(following["keeps"]))
                def _():
                    for j in range(2):
                        mate_send(k + 1, j, following["target"]).wait_send()
                        cross_copy(k + 1, j, following["partner"]).wait_send()

            y_copy(k, partner).start()

        return carry

    lax.fori_loop(0, top, up, 0)

    def forward_y(k, carry):
        r = roles(k)

        @pl.when(r["active"])
        def _():
            y_copy(k, r["partner"]).wait_recv()
            y_forward(k).start()

        return carry

    lax.fori_loop(0, top - 1, forward_y, 0)

    r_top = roles(top)

    @pl.when(r_top["active"])
    def _():
        cross_copy(top, 0, r_top["partner"]).wait_recv()
        cross_forward(top, 0).start()
        source_copy(top, 0, r_top["partner"]).wait_recv()
        mate_copy(top, 0, other_half).wait_recv()
        mate_near = split(mate[top, 0])
        rhs = gs[top, 0] - mm(split(goth[top, 0]), mate_near)
        cross_forward(top, 0, other_half).wait_recv()
        cross_near = split(cross[top, 0])
        coupling = mm(cross_near, mate_near)
        middle = refined(rhs, approx_rest(coupling), split(coupling))
        t = goth[top, 0] - mm(split(middle), cross_near)
        ebuf[top, 0] = jnp.zeros_like(t)
        esrc[top] = t
        new_edge_copy(top, 1, r_top["retiree"]).start()
        old_edge_copy(top, 1, r_top["retiree"]).start()
        ebuf[top - 1, 0] = t
        ebuf[top - 1, 1] = jnp.zeros_like(t)

    forward_y(top - 1, 0)

    def down(index, carry):
        k = top - 1 - index
        r = roles(k)
        above = roles(k + 1)
        keep = r["keep"]

        @pl.when(r["active"])
        def _():
            z_copy(k, other_half).wait_recv()
            y_forward(k, other_half).wait_recv()
            for part, rec in enumerate((zrec, yrec)):
                high, low = split(rec[k])
                rec_high[part * block : (part + 1) * block] = high
                rec_low[part * block : (part + 1) * block] = low

            @pl.when(above["retiring"])
            def _():
                old_edge_copy(k + 1, above["keep"], s).wait_recv()
                new_edge_copy(k + 1, above["keep"], s).wait_recv()

            @pl.when(k > 0)
            def _():
                old_edge_copy(k, keep, r["retiree"]).start()

            own_edge = ebuf[k, 0]
            high, low = split(jnp.concatenate([own_edge, -ebuf[k, 1]], axis=1))
            columns = own_edge.shape[0]
            stacked = dot(jnp.concatenate([high, low], axis=0), rec_high[...])
            new = trec[k] + (
                stacked[:columns] + (stacked[columns:] + dot(high, rec_low[...]))
            )

            @pl.when(k > 0)
            def _():
                esrc[k] = new
                new_edge_copy(k, keep, r["retiree"]).start()
                ebuf[k - 1, 1 - keep] = new
                ebuf[k - 1, keep] = own_edge

            @pl.when(k == 0)
            def _():
                out[h0] = own_edge
                out[1 - h0] = new

        return carry

    lax.fori_loop(0, top, down, 0)

    def finish(k, carry):
        r = roles(k)
        keeps = r["keeps"]
        below_top = k < top
        sends_cross = jnp.logical_or(
            both(r["active"], keeps), both(r["retiring"], jnp.logical_not(keeps))
        )

        @pl.when(sends_cross)
        def _():
            source_copy(k, 0, r["partner"]).wait_send()

            @pl.when(below_top)
            def _():
                source_copy(k, 1, r["partner"]).wait_send()

        @pl.when(both(r["active"], keeps))
        def _():
            cross_copy(k, 0, r["partner"]).wait_send()

            @pl.when(below_top)
            def _():
                cross_copy(k, 1, r["partner"]).wait_send()

        @pl.when(r["active"])
        def _():
            cross_forward(k, 0).wait_send()

            @pl.when(k > 0)
            def _():
                mate_copy(k, 0).wait_send()
                old_edge_copy(k, r["keep"], r["retiree"]).wait_send()
                new_edge_copy(k, r["keep"], r["retiree"]).wait_send()

            @pl.when(below_top)
            def _():
                cross_forward(k, 1).wait_send()
                z_copy(k).wait_send()
                y_copy(k, r["partner"]).wait_send()
                y_forward(k).wait_send()

            @pl.when(both(k > 0, below_top))
            def _():
                mate_copy(k, 1).wait_send()

        return carry

    lax.fori_loop(0, levels, finish, 0)


def local(right_spike, left_spike, local_rhs):
    block = right_spike.shape[1]
    part_rows = right_spike.shape[0]
    columns = local_rhs.shape[0]
    levels = lax.axis_size("slab").bit_length() - 1
    last = part_rows - block
    tips = jnp.stack(
        [left_spike[:block].T, left_spike[last:].T, right_spike[last:].T, right_spike[:block].T]
    )
    sources = jnp.stack([local_rhs[:, :block], local_rhs[:, last:]])
    half = block // 2
    f32 = jnp.float32
    pair = pltpu.SemaphoreType.DMA((levels, 2))
    one = pltpu.SemaphoreType.DMA((levels,))
    vmem = pl.BlockSpec(memory_space=pltpu.VMEM)
    edges = pl.pallas_call(
        functools.partial(kernel, levels),
        out_shape=jax.ShapeDtypeStruct((2, columns, block), f32),
        in_specs=[vmem, vmem],
        out_specs=vmem,
        scratch_shapes=[
            pltpu.VMEM((levels, 2, half, block), f32),
            pltpu.VMEM((levels, 2, block, block), f32),
            pltpu.VMEM((levels, 2, block, block), f32),
            pltpu.VMEM((levels, 2, half, block), f32),
            pltpu.VMEM((levels, 2, columns, block), f32),
            pltpu.VMEM((levels, 2, columns, block), f32),
            pltpu.VMEM((levels, block, block), f32),
            pltpu.VMEM((levels, block, block), f32),
            pltpu.VMEM((levels, half, block), f32),
            pltpu.VMEM((levels, columns, block), f32),
            pltpu.VMEM((levels, 2, columns, block), f32),
            pltpu.VMEM((levels, columns, block), f32),
            pltpu.VMEM((2 * block, block), jnp.bfloat16),
            pltpu.VMEM((2 * block, block), jnp.bfloat16),
            pltpu.VMEM((2, block, block), jnp.bfloat16),
            pltpu.VMEM((2, block, block), jnp.bfloat16),
        ]
        + [pair] * 15
        + [one] * 6,
        compiler_params=pltpu.CompilerParams(
            collective_id=0, has_side_effects=True, vmem_limit_bytes=40 * 2**20
        ),
    )(tips, sources)

    def against(rows, matrix):
        return lax.dot_general(
            rows,
            matrix,
            (((1,), (1,)), ((), ())),
            precision=lax.Precision.HIGH,
            preferred_element_type=f32,
        )

    return local_rhs - against(edges[1], right_spike) - against(edges[0], left_spike)


def solution(mesh):
    return jax.shard_map(
        local,
        mesh=mesh,
        in_specs=(P("slab", None), P("slab", None), P("rhs", "slab")),
        out_specs=P("rhs", "slab"),
        check_vma=False,
    )
```

```python
import functools
import jax
import jax.numpy as jnp
from jax import lax
from jax.experimental import pallas as pl
from jax.experimental.pallas import tpu as pltpu
from jax.sharding import PartitionSpec as P

MESH = pl.DeviceIdType.MESH


def split(x):
    high = x.astype(jnp.bfloat16)
    return high, (x - high.astype(jnp.float32)).astype(jnp.bfloat16)


def mm(left, right):
    left_high, left_low = left
    right_high, right_low = right
    return jnp.dot(
        jnp.concatenate([left_high, left_high, left_low], axis=1),
        jnp.concatenate([right_high, right_low, right_high], axis=0),
        preferred_element_type=jnp.float32,
    )


def places(levels, left_level, outer_level):
    p = q = 0
    rows = []
    for k in range(levels):
        d = 2**k
        if k == left_level and k < levels - 1:
            rows.append((d, p, p, q, q, 0, 1))
            p, q = p, d + p
        elif k == outer_level and k < levels - 1:
            rows.append((d, p, q, q, p, 0, 0))
            p, q = p, d + q
        else:
            rows.append((d, q, p, p, q, 1, 1))
            p, q = q, d + p
    return rows


LEFT_LEVEL = 2
OUTER_LEVEL = 6


def kernel(
    levels, tips, sources, out,
    side, mate, cross, own, gs, goth, zrec, yrec, ysrc, trec, ebuf, esrc, rec_high, rec_low,
    mate_high, mate_low,
    msend, mrecv, tsend, trecv, csend, crecv, fsend, frecv, osend, orecv, gsend, grecv,
    esend, erecv, kept_sem, zsend, zrecv, ysend, yrecv, vsend, vrecv,
):
    s = lax.axis_index("slab")
    c = lax.axis_index("rhs")
    o = 1 - c
    block = tips.shape[1]
    half_size = block // 2
    half = pl.ds(pl.multiple_of(c * half_size, half_size), half_size)
    other_half = pl.ds(pl.multiple_of(o * half_size, half_size), half_size)
    top = levels - 1
    rows_of = places(levels, LEFT_LEVEL, OUTER_LEVEL)

    def table(k, column):
        values = [row[column] for row in rows_of]
        if isinstance(k, int):
            return values[k]
        value = jnp.int32(values[0])
        for i in range(1, levels):
            value = jnp.where(k == i, values[i], value)
        return value

    def roles(k):
        d, act0, act1, ret0, ret1, keep0, keep1 = [table(k, i) for i in range(7)]
        off = lax.rem(s, d)
        h = lax.rem(lax.div(s, d), 2)
        act_off = act0 + h * (act1 - act0)
        ret_off = ret0 + h * (ret1 - ret0)
        keep = keep0 + h * (keep1 - keep0)
        base = s - off
        other = base + (1 - 2 * h) * d
        return {
            "active": off == act_off,
            "retiring": jnp.logical_and(off == ret_off, act_off != ret_off),
            "keep": keep,
            "keeps": keep == 1,
            "target": base + act_off,
            "retiree": base + ret_off,
            "partner": other + act1 + h * (act0 - act1),
            "other_retiree": other + ret1 + h * (ret0 - ret1),
        }

    def both(*conditions):
        return functools.reduce(jnp.logical_and, conditions)

    def remote(src, dst, send, recv, slab, core):
        return pltpu.make_async_remote_copy(
            src_ref=src, dst_ref=dst, send_sem=send, recv_sem=recv,
            device_id=(slab, core), device_id_type=MESH,
        )

    def mate_copy(k, j, rows=half):
        ref = mate.at[k, j, rows]
        return remote(ref, ref, msend.at[k, j], mrecv.at[k, j], s, o)

    def mate_send(k, j, target):
        return remote(
            side.at[k, j], mate.at[k, j, half], tsend.at[k, j], trecv.at[k, j], target, c
        )

    def cross_copy(k, j, partner):
        return remote(
            side.at[k, j], cross.at[k, j, half], csend.at[k, j], crecv.at[k, j], partner, c
        )

    def cross_forward(k, j, rows=half):
        ref = cross.at[k, j, rows]
        return remote(ref, ref, fsend.at[k, j], frecv.at[k, j], s, o)

    def own_copy(k, j, target):
        return remote(side.at[k, j], own.at[k, j], osend.at[k, j], orecv.at[k, j], target, c)

    def own_keep(k, j):
        return pltpu.make_async_copy(side.at[k, j], own.at[k, j], kept_sem.at[k, j])

    def source_copy(k, j, partner):
        return remote(gs.at[k, j], goth.at[k, j], gsend.at[k, j], grecv.at[k, j], partner, c)

    def z_copy(k, rows=half):
        ref = zrec.at[k, rows]
        return remote(ref, ref, zsend.at[k], zrecv.at[k], s, o)

    def y_copy(k, partner):
        return remote(ysrc.at[k], yrec.at[k, half], ysend.at[k], yrecv.at[k], partner, c)

    def y_forward(k, rows=half):
        ref = yrec.at[k, rows]
        return remote(ref, ref, vsend.at[k], vrecv.at[k], s, o)

    def old_edge_copy(k, keep, target):
        return remote(
            ebuf.at[k, 0], ebuf.at[k - 1, 1 - keep], esend.at[k, 0], erecv.at[k, 0], target, c
        )

    def new_edge_copy(k, keep, target):
        return remote(
            esrc.at[k], ebuf.at[k - 1, keep], esend.at[k, 1], erecv.at[k, 1], target, c
        )

    barrier = pltpu.get_barrier_semaphore()

    def greet(slab, core):
        pl.semaphore_signal(barrier, inc=1, device_id=(slab, core), device_id_type=MESH)

    greet(s, o)
    greet(roles(0)["partner"], c)
    greeted = 2
    for k in range(1, levels):
        r = roles(k)

        @pl.when(r["active"])
        def _():
            greet(r["retiree"], c)

        @pl.when(r["retiring"])
        def _():
            greet(r["target"], c)

        takes_part = jnp.logical_or(r["active"], r["retiring"])

        @pl.when(takes_part)
        def _():
            greet(r["partner"], c)
            greet(r["other_retiree"], c)

        greeted = greeted + jnp.where(takes_part, 3, 0)

    h0 = lax.rem(s, 2)
    for j in range(2):
        mate[0, j] = tips[2 * (1 - h0) + j]
        side[0, j] = tips[2 * (1 - h0) + j, half]
        own[0, j] = tips[2 * h0 + j, half]
    gs[0, 0] = sources[1 - h0]
    gs[0, 1] = sources[h0]
    pl.semaphore_wait(barrier, greeted)

    first_partner = roles(0)["partner"]
    cross_copy(0, 0, first_partner).start()
    for j in range(2):
        source_copy(0, j, first_partner).start()

    dot = functools.partial(jnp.dot, preferred_element_type=jnp.float32)

    def approx_rest(coupling):
        first = coupling.astype(jnp.bfloat16)
        square = dot(first, first)
        second = square.astype(jnp.bfloat16)
        rest = coupling + square + dot(first, second)
        fourth = dot(second, second)
        rest = rest + fourth + dot(rest.astype(jnp.bfloat16), fourth.astype(jnp.bfloat16))
        return rest.astype(jnp.bfloat16)

    def refined(rows, rest, coupling):
        start = rows + dot(rows.astype(jnp.bfloat16), rest)
        residual = (rows - start) + mm(split(start), coupling)
        return start + (residual + dot(residual.astype(jnp.bfloat16), rest))

    def send_side(k, j, r, value):
        below_top = k < top
        retiring = r["retiring"] if j == 0 else both(r["retiring"], below_top)
        active = r["active"] if j == 0 else both(r["active"], below_top)
        keeps = r["keeps"]

        @pl.when(both(active, keeps))
        def _():
            if j == 0:
                cross_copy(k, j, r["partner"]).start()
            mate[k, j, half] = value
            mate_copy(k, j).start()
            source_copy(k, j, r["partner"]).start()

        @pl.when(both(active, jnp.logical_not(keeps)))
        def _():
            own_keep(k, j).start()

        @pl.when(both(retiring, keeps, below_top))
        def _():
            own_copy(k, j, r["target"]).start()

        @pl.when(both(retiring, jnp.logical_not(keeps)))
        def _():
            mate_send(k, j, r["target"]).start()
            cross_copy(k, j, r["partner"]).start()
            source_copy(k, j, r["partner"]).start()

    def up(k, carry):
        r = roles(k)
        following = roles(k + 1)
        keep = r["keep"]
        partner = r["partner"]
        retiree = r["retiree"]
        moved = both(k > 0, jnp.logical_not(r["keeps"]))
        kept = both(k > 0, r["keeps"])

        def split_mate(j):
            mate_high[j], mate_low[j] = split(mate[k, j])

        @pl.when(r["active"])
        def _():
            @pl.when(moved)
            def _():
                mate_send(k, 0, r["target"]).wait_recv()
                mate_copy(k, 0).start()

            @pl.when(k > 0)
            def _():
                mate_copy(k, 0, other_half).wait_recv()

            split_mate(0)

            @pl.when(kept)
            def _():
                mate_copy(k, 1, other_half).wait_recv()

            @pl.when(jnp.logical_not(moved))
            def _():
                split_mate(1)

            cross_copy(k, 0, partner).wait_recv()
            cross_forward(k, 0).start()

            @pl.when(r["keeps"])
            def _():
                cross_copy(k, 1, partner).start()

            @pl.when(k > 0)
            def _():
                y_copy(k - 1, roles(jnp.maximum(k - 1, 0))["partner"]).start()

            source_copy(k, 0, partner).wait_recv()
            mate_near = mate_high[0], mate_low[0]
            rhs = gs[k, 1 - keep] - mm(split(goth[k, 0]), mate_near)
            cross_forward(k, 0, other_half).wait_recv()
            cross_near = split(cross[k, 0])
            coupling = mm(cross_near, mate_near)
            rest = approx_rest(coupling)
            coupling = split(coupling)

            @pl.when(kept)
            def _():
                own_copy(k, 1, retiree).wait_recv()

            @pl.when(moved)
            def _():
                own_keep(k, 1).wait()

            rows = jnp.concatenate([own[k, 1], rhs], axis=0)
            y = refined(rows, rest, coupling)
            y_parts = split(y)
            cross_copy(k, 1, partner).wait_recv()
            cross_forward(k, 1).start()
            z = mm(y_parts, cross_near)
            z_own = z[:half_size]
            t = goth[k, 0] - z[half_size:]

            @pl.when(moved)
            def _():
                mate_send(k, 1, r["target"]).wait_recv()
                mate_copy(k, 1).start()
                own_keep(k, 0).wait()
                mate_copy(k, 1, other_half).wait_recv()
                split_mate(1)

            @pl.when(kept)
            def _():
                own_copy(k, 0, retiree).wait_recv()

            near = jnp.concatenate([own[k, 0], gs[k, keep]], axis=0) + mm(
                split(jnp.concatenate([z_own, -t], axis=0)), (mate_high[1], mate_low[1])
            )
            side[k + 1, 0] = near[:half_size]
            gs[k + 1, 0] = near[half_size:]
            send_side(k + 1, 0, following, near[:half_size])

            trec[k] = t
            ysrc[k] = y[:half_size]
            zrec[k, half] = z_own
            source_copy(k, 1, partner).wait_recv()
            cross_forward(k, 1, other_half).wait_recv()
            product = mm(y_parts, split(cross[k, 1]))
            side[k + 1, 1] = -product[:half_size]
            gs[k + 1, 1] = goth[k, 1] - product[half_size:]
            send_side(k + 1, 1, following, -product[:half_size])
            z_copy(k).start()

            @pl.when(both(following["retiring"], k + 1 < top))
            def _():
                @pl.when(following["keeps"])
                def _():
                    for j in range(2):
                        own_copy(k + 1, j, following["target"]).wait_send()

                @pl.when(jnp.logical_not(following["keeps"]))
                def _():
                    for j in range(2):
                        mate_send(k + 1, j, following["target"]).wait_send()
                        cross_copy(k + 1, j, following["partner"]).wait_send()

            @pl.when(following["retiring"])
            def _():
                y_copy(k, partner).start()

        return carry

    lax.fori_loop(0, top, up, 0)

    def forward_y(k, carry):
        r = roles(k)

        @pl.when(r["active"])
        def _():
            y_copy(k, r["partner"]).wait_recv()
            y_forward(k).start()

        return carry

    lax.fori_loop(0, top - 1, forward_y, 0)

    r_top = roles(top)

    @pl.when(r_top["active"])
    def _():
        cross_copy(top, 0, r_top["partner"]).wait_recv()
        cross_forward(top, 0).start()
        y_copy(top - 1, roles(top - 1)["partner"]).start()
        source_copy(top, 0, r_top["partner"]).wait_recv()
        mate_copy(top, 0, other_half).wait_recv()
        mate_near = split(mate[top, 0])
        rhs = gs[top, 0] - mm(split(goth[top, 0]), mate_near)
        cross_forward(top, 0, other_half).wait_recv()
        cross_near = split(cross[top, 0])
        coupling = mm(cross_near, mate_near)
        middle = refined(rhs, approx_rest(coupling), split(coupling))
        t = goth[top, 0] - mm(split(middle), cross_near)
        ebuf[top, 0] = jnp.zeros_like(t)
        esrc[top] = t
        new_edge_copy(top, 1, r_top["retiree"]).start()
        old_edge_copy(top, 1, r_top["retiree"]).start()
        ebuf[top - 1, 0] = t
        ebuf[top - 1, 1] = jnp.zeros_like(t)

    forward_y(top - 1, 0)

    def down(index, carry):
        k = top - 1 - index
        r = roles(k)
        above = roles(k + 1)
        keep = r["keep"]

        @pl.when(r["active"])
        def _():
            z_copy(k, other_half).wait_recv()
            y_forward(k, other_half).wait_recv()
            for part, rec in enumerate((zrec, yrec)):
                high, low = split(rec[k])
                rec_high[part * block : (part + 1) * block] = high
                rec_low[part * block : (part + 1) * block] = low

            @pl.when(above["retiring"])
            def _():
                old_edge_copy(k + 1, above["keep"], s).wait_recv()
                new_edge_copy(k + 1, above["keep"], s).wait_recv()

            @pl.when(k > 0)
            def _():
                old_edge_copy(k, keep, r["retiree"]).start()

            own_edge = ebuf[k, 0]
            high, low = split(jnp.concatenate([own_edge, -ebuf[k, 1]], axis=1))
            columns = own_edge.shape[0]
            stacked = dot(jnp.concatenate([high, low], axis=0), rec_high[...])
            new = trec[k] + (
                stacked[:columns] + (stacked[columns:] + dot(high, rec_low[...]))
            )

            @pl.when(k > 0)
            def _():
                esrc[k] = new
                new_edge_copy(k, keep, r["retiree"]).start()
                ebuf[k - 1, 1 - keep] = new
                ebuf[k - 1, keep] = own_edge

            @pl.when(k == 0)
            def _():
                out[h0] = own_edge
                out[1 - h0] = new

        return carry

    lax.fori_loop(0, top, down, 0)

    def finish(k, carry):
        r = roles(k)
        keeps = r["keeps"]
        below_top = k < top
        sends_cross = jnp.logical_or(
            both(r["active"], keeps), both(r["retiring"], jnp.logical_not(keeps))
        )

        @pl.when(sends_cross)
        def _():
            source_copy(k, 0, r["partner"]).wait_send()

            @pl.when(below_top)
            def _():
                source_copy(k, 1, r["partner"]).wait_send()

        @pl.when(both(r["active"], keeps))
        def _():
            cross_copy(k, 0, r["partner"]).wait_send()

            @pl.when(below_top)
            def _():
                cross_copy(k, 1, r["partner"]).wait_send()

        @pl.when(r["active"])
        def _():
            cross_forward(k, 0).wait_send()

            @pl.when(k > 0)
            def _():
                mate_copy(k, 0).wait_send()
                old_edge_copy(k, r["keep"], r["retiree"]).wait_send()
                new_edge_copy(k, r["keep"], r["retiree"]).wait_send()

            @pl.when(below_top)
            def _():
                cross_forward(k, 1).wait_send()
                z_copy(k).wait_send()
                y_copy(k, r["partner"]).wait_send()
                y_forward(k).wait_send()

            @pl.when(both(k > 0, below_top))
            def _():
                mate_copy(k, 1).wait_send()

        return carry

    lax.fori_loop(0, levels, finish, 0)


def local(right_spike, left_spike, local_rhs):
    block = right_spike.shape[1]
    part_rows = right_spike.shape[0]
    columns = local_rhs.shape[0]
    levels = lax.axis_size("slab").bit_length() - 1
    last = part_rows - block
    tips = jnp.stack(
        [left_spike[:block].T, left_spike[last:].T, right_spike[last:].T, right_spike[:block].T]
    )
    sources = jnp.stack([local_rhs[:, :block], local_rhs[:, last:]])
    half = block // 2
    f32 = jnp.float32
    pair = pltpu.SemaphoreType.DMA((levels, 2))
    one = pltpu.SemaphoreType.DMA((levels,))
    vmem = pl.BlockSpec(memory_space=pltpu.VMEM)
    edges = pl.pallas_call(
        functools.partial(kernel, levels),
        out_shape=jax.ShapeDtypeStruct((2, columns, block), f32),
        in_specs=[vmem, vmem],
        out_specs=vmem,
        scratch_shapes=[
            pltpu.VMEM((levels, 2, half, block), f32),
            pltpu.VMEM((levels, 2, block, block), f32),
            pltpu.VMEM((levels, 2, block, block), f32),
            pltpu.VMEM((levels, 2, half, block), f32),
            pltpu.VMEM((levels, 2, columns, block), f32),
            pltpu.VMEM((levels, 2, columns, block), f32),
            pltpu.VMEM((levels, block, block), f32),
            pltpu.VMEM((levels, block, block), f32),
            pltpu.VMEM((levels, half, block), f32),
            pltpu.VMEM((levels, columns, block), f32),
            pltpu.VMEM((levels, 2, columns, block), f32),
            pltpu.VMEM((levels, columns, block), f32),
            pltpu.VMEM((2 * block, block), jnp.bfloat16),
            pltpu.VMEM((2 * block, block), jnp.bfloat16),
            pltpu.VMEM((2, block, block), jnp.bfloat16),
            pltpu.VMEM((2, block, block), jnp.bfloat16),
        ]
        + [pair] * 15
        + [one] * 6,
        compiler_params=pltpu.CompilerParams(
            collective_id=0, has_side_effects=True, vmem_limit_bytes=40 * 2**20
        ),
    )(tips, sources)

    def against(rows, matrix):
        return lax.dot_general(
            rows,
            matrix,
            (((1,), (1,)), ((), ())),
            precision=lax.Precision.HIGH,
            preferred_element_type=f32,
        )

    return local_rhs - against(edges[1], right_spike) - against(edges[0], left_spike)


def solution(mesh):
    return jax.shard_map(
        local,
        mesh=mesh,
        in_specs=(P("slab", None), P("slab", None), P("rhs", "slab")),
        out_specs=P("rhs", "slab"),
        check_vma=False,
    )
```
